32 devices in a mesh: groups: 2 (over y), space: 4 (over z), mode: 4 (over x, core).
Axes of the slice: x: 2, y: 2, z: 4, core: 2. Of those that a mesh axis runs over, the one named last changes fastest.
Arguments:
- new_modes: bfloat16 [16, 3, 16, 16, 128], P(('groups', 'mode'), None, 'space'), parts along dimension 0, may hold values from -6 to 6
- phase_ids: int32 [32, 16, 128], P(('groups', 'space')), parts along dimension 0, may hold values 0 or 1
- stiffness_table: float32 [2, 27, 3, 3], replicated, may hold values from -0.625 to 0.625
- mode_basis: bfloat16 [1024, 3, 16, 16, 128], P(('groups', 'mode'), None, 'space'), parts along dimension 0, may hold values from -0.01953125 to 0.01953125
Outputs:
- images: bfloat16 [16, 3, 16, 16, 128], P(('groups', 'mode'), None, 'space'), parts along dimension 0
- galerkin: float32 [1024, 8], P(('groups', 'mode')), parts along dimension 0
The draws below stay inside these ranges and needn't reach their ends.
There are 2 independent parts, one for each index of `groups`. The reference program is written for one: setup_inputs(seed, part) draws one part's arguments, and reference() takes and returns one part's arrays. A program takes and returns all parts, laid end to end along the dimension named above; an argument that names none is the same for every part. Nothing has to cross between parts.
All inputs are finite; a program needn't handle non-finite values. No bound on the sum of `phase_ids` on one device may be relied on, other than what follows from the above.
Results may differ from the reference program's by a relative error of at most 0.0028.
Values may be sent and summed in bfloat16 or wider, within the bound.
A program may use at most 64 MiB of HBM per device.

```python
import jax
import jax.numpy as jnp
from jax import lax

MODES = 512
NEW = 8
NX = 16
NY = 128
NZ = 16


def set_ends(result, rng, least, high):
    longest = result.shape.index(max(result.shape))
    spots = []
    for shift in (0, 1):
        where = [jax.random.randint(jax.random.fold_in(rng, axis), (), 0, length) for axis, length in enumerate(result.shape)]
        where[longest] = (where[longest] + shift) % result.shape[longest]
        spots.append(tuple(where))
    return result.at[spots[0]].set(least).at[spots[1]].set(high)


def level_of(rng, extent, cuts, low, high):
    def one(axis_at, blocks):
        heights = jax.random.uniform(jax.random.fold_in(jax.random.fold_in(rng, 6), axis_at), (blocks,), jnp.float32, low / len(cuts), high / len(cuts))
        return jnp.repeat(jnp.exp(heights), extent[axis_at] // blocks).reshape((-1,) + (1,) * (len(extent) - axis_at - 1))

    loudness = one(*cuts[0])
    for cut in cuts[1:]:
        loudness = loudness * one(*cut)
    return loudness


def scatter_about(stream_key, extent, width, bound, pieces=(), held_as=jnp.bfloat16):
    entries = width * jax.random.normal(stream_key, extent, jnp.float32)
    if pieces:
        entries = entries * level_of(stream_key, extent, pieces, -0.22, 0.18)
    return jnp.clip(entries, -bound, bound).astype(held_as)


def setup_inputs(seed: int = 0, part: int = 0) -> dict:
    seeds = jax.random.split(jax.random.key(seed), 5)
    own_keys = jax.random.split(jax.random.fold_in(seeds[4], part), 5)
    new_modes = scatter_about(own_keys[0], (NEW, 3, NZ, NX, NY), 1.0, 6.0, ((0, 4), (2, 4)))
    phase_ids = set_ends((jax.random.randint(own_keys[1], (NZ, NX, NY), 0, 3) < 1).astype(jnp.int32), jax.random.fold_in(own_keys[1], 1), 0, 1)
    stiffness_table = scatter_about(seeds[2], (2, 27, 3, 3), 81 ** -0.5, 0.625, (), jnp.float32)
    mode_basis = scatter_about(own_keys[3], (MODES, 3, NZ, NX, NY), (3 * NX * NY * NZ) ** -0.5, 0.01953125, ((0, 4), (2, 4)))
    return {"new_modes": new_modes, "phase_ids": phase_ids, "stiffness_table": stiffness_table, "mode_basis": mode_basis}


def apply_stiffness(field, phase_f, stiffness_table):
    outputs = [jnp.zeros(field[:, 0].shape, jnp.float32) for comp in range(3)]
    for step_z in (-1, 0, 1):
        for step_x in (-1, 0, 1):
            for step_y in (-1, 0, 1):
                column = 9 * (step_z + 1) + 3 * (step_x + 1) + (step_y + 1)
                shifted = jnp.roll(field, (-step_z, -step_x, -step_y), axis=(2, 3, 4))
                for row in range(3):
                    for inner in range(3):
                        base_coef = stiffness_table[0, column, row, inner]
                        delta_coef = stiffness_table[1, column, row, inner] - base_coef
                        coefficient = base_coef + delta_coef * phase_f
                        outputs[row] = outputs[row] + coefficient[None] * shifted[:, inner]
    return jnp.stack(outputs, axis=1)


def reference(new_modes, phase_ids, stiffness_table, mode_basis):
    phase_f = phase_ids.astype(jnp.float32)
    images = apply_stiffness(new_modes.astype(jnp.float32), phase_f, stiffness_table).astype(jnp.bfloat16)
    galerkin = lax.dot_general(mode_basis.reshape(mode_basis.shape[0], -1), images.reshape(images.shape[0], -1), (((1,), (1,)), ((), ())), preferred_element_type=jnp.float32)
    return images, galerkin
```

```python
import functools

import jax
import jax.numpy as jnp
from jax import lax
from jax.experimental import pallas as pl
from jax.experimental.pallas import tpu as pltpu
from jax.sharding import PartitionSpec as P

MESH = pl.DeviceIdType.MESH
NT = (((1,), (1,)), ((), ()))


def kernel(
    space, mode, tile,
    modes_hbm, phase_hbm, table_hbm, basis_hbm, images_hbm, rows_ref,
    padded, phase, table, basis, band_hi, band_lo, gathered, own, product, picked, partial,
    load_sem, basis_sem, halo_send, halo_recv, image_send, image_recv, core_send, core_recv,
    pass_send, pass_recv, sum_send, sum_recv, out_sem,
):
    fresh, _, depth, width, _ = modes_hbm.shape
    count = basis_hbm.shape[0]
    chips = mode // 2
    me_space = lax.axis_index("space")
    me = lax.axis_index("mode")
    chip, core = me // 2, lax.rem(me, 2)
    sibling = chip * 2 + (1 - core)
    across = [lax.rem(chip + k, chips) * 2 + core for k in range(1, chips)]
    behind = [lax.rem(chip + chips - k, chips) * 2 + core for k in range(1, chips)]
    up = lax.rem(me_space + 1, space)
    down = lax.rem(me_space + space - 1, space)
    order = list(range(1, depth - 1)) + [0, depth - 1]
    passes = [order[k : k + 2] for k in range(0, depth, 2)]

    load_table = pltpu.make_async_copy(table_hbm, table, load_sem.at[0])
    load_modes = pltpu.make_async_copy(modes_hbm, padded.at[:, :, pl.ds(1, depth)], load_sem.at[1])
    load_phase = pltpu.make_async_copy(phase_hbm, phase, load_sem.at[2])
    load_table.start()
    load_modes.start()
    load_phase.start()

    barrier = pltpu.get_barrier_semaphore()
    for k in range(1, space):
        pl.semaphore_signal(
            barrier, inc=1, device_id={"space": lax.rem(me_space + k, space)}, device_id_type=MESH
        )
    for peer in across + [sibling]:
        pl.semaphore_signal(barrier, inc=1, device_id={"mode": peer}, device_id_type=MESH)

    load_basis = pltpu.make_async_copy(basis_hbm, basis, basis_sem)
    load_basis.start()

    load_table.wait()
    columns = 9 * width
    lane = lax.broadcasted_iota(jnp.int32, (width, columns), 1)
    row = lax.broadcasted_iota(jnp.int32, (width, columns), 0)
    block = lane // width
    offset = lax.rem(lane - row + columns + 1, width)

    def build(q, carry):
        step_y, which, comp = q // 6, lax.rem(q // 3, 2), lax.rem(q, 3)
        total = jnp.zeros((width, columns), jnp.float32)
        for step_x in range(3):
            value = jnp.zeros((width, columns), jnp.float32)
            for inner in range(3):
                for step_z in range(3):
                    coef = table[comp, inner, which, 9 * step_z + 3 * step_x + step_y]
                    value = jnp.where(block == 3 * inner + step_z, coef, value)
            total = jnp.where(offset == step_x, value, total)
        high = total.astype(jnp.bfloat16)
        at = pl.ds(pl.multiple_of(q * width, width), width)
        band_hi[at, :] = high
        band_lo[at, :] = (total - high.astype(jnp.float32)).astype(jnp.bfloat16)
        return carry

    lax.fori_loop(0, 18, build, 0)

    pl.semaphore_wait(barrier, space - 1 + len(across) + 1)

    halos = []
    for side, (layer, target, slot) in enumerate(((depth - 1, up, 0), (0, down, depth + 1))):
        copy = pltpu.make_async_remote_copy(
            src_ref=modes_hbm.at[:, :, pl.ds(layer, 1)],
            dst_ref=padded.at[:, :, pl.ds(slot, 1)],
            send_sem=halo_send.at[side],
            recv_sem=halo_recv.at[side],
            device_id={"space": target},
            device_id_type=MESH,
        )
        copy.start()
        halos.append(copy)

    load_modes.wait()
    load_phase.wait()

    sends = []

    def layer_images(z):
        field = jnp.concatenate(
            [padded[n, :, z : z + 3].reshape(columns, 128) for n in range(fresh)], axis=1
        )
        sums = jnp.dot(band_hi[...], field, preferred_element_type=jnp.float32)
        sums = sums + jnp.dot(band_lo[...], field, preferred_element_type=jnp.float32)
        ids = phase[z]
        masks = [pltpu.roll(ids, shift, 1) == 1 if shift else ids == 1 for shift in (127, 0, 1)]
        for n in range(fresh):
            for comp in range(3):
                result = None
                for step_y, back in ((1, 0), (0, 1), (2, 127)):
                    first = (6 * step_y + comp) * width
                    second = first + 3 * width
                    lanes = slice(n * 128, (n + 1) * 128)
                    term = jnp.where(
                        masks[step_y], sums[second : second + width, lanes], sums[first : first + width, lanes]
                    )
                    term = pltpu.roll(term, back, 1) if back else term
                    result = term if result is None else result + term
                image = result.astype(jnp.bfloat16)
                gathered[me, z, comp, n] = image
                own[n, comp, z] = image

    def send_layer(z):
        spot = gathered.at[me, pl.ds(z, 1)]
        for k, peer in enumerate(across):
            copy = pltpu.make_async_remote_copy(
                src_ref=spot, dst_ref=spot, send_sem=image_send.at[z, k], recv_sem=image_recv.at[z, k],
                device_id={"mode": peer}, device_id_type=MESH,
            )
            copy.start()
            sends.append(copy)
        copy = pltpu.make_async_remote_copy(
            src_ref=spot, dst_ref=spot, send_sem=core_send.at[z], recv_sem=core_recv.at[z],
            device_id={"mode": sibling}, device_id_type=MESH,
        )
        copy.start()
        sends.append(copy)

    def arrived(spot, sem):
        pltpu.make_async_remote_copy(
            src_ref=spot, dst_ref=spot, send_sem=out_sem, recv_sem=sem,
            device_id={"mode": sibling}, device_id_type=MESH,
        ).wait_recv()

    def pass_layer(z):
        for k, source in enumerate(behind):
            spot = gathered.at[source, pl.ds(z, 1)]
            arrived(spot, image_recv.at[z, k])
            copy = pltpu.make_async_remote_copy(
                src_ref=spot, dst_ref=spot, send_sem=pass_send.at[z, k], recv_sem=pass_recv.at[z, k],
                device_id={"mode": sibling}, device_id_type=MESH,
            )
            copy.start()
            sends.append(copy)

    for z in order:
        if z == 0:
            for copy in halos:
                copy.wait_recv()
        layer_images(z)
        send_layer(z)

    store_images = pltpu.make_async_copy(own, images_hbm, load_sem.at[3])
    store_images.start()

    lanes = fresh * mode * width
    spread = lax.broadcasted_iota(jnp.int32, (width, lanes), 1)
    keep = lax.rem(spread, width) == lax.broadcasted_iota(jnp.int32, (width, lanes), 0)
    for z in order:
        pass_layer(z)
    load_basis.wait()
    for number, layers in enumerate(passes):
        for z in layers:
            arrived(gathered.at[sibling, pl.ds(z, 1)], core_recv.at[z])
            for k, source in enumerate(behind):
                other = source + 1 - 2 * core
                arrived(gathered.at[other, pl.ds(z, 1)], pass_recv.at[z, k])

        def multiply(t, carry):
            at = pl.ds(t * tile, tile)
            left = jnp.concatenate(
                [basis[at, c, z].reshape(tile * width, 128) for z in layers for c in range(3)], axis=1
            )
            right = jnp.concatenate(
                [gathered[:, z, c].reshape(lanes, 128) for z in layers for c in range(3)], axis=1
            )
            value = lax.dot_general(left, right, NT, preferred_element_type=jnp.float32)
            if number > 0:
                value = value + product[t]
            if number < len(passes) - 1:
                product[t] = value
            else:
                cut = jnp.where(keep[None], value.reshape(tile, width, lanes), 0.0)
                picked[pl.ds(pl.multiple_of(t * tile, tile), tile), :] = jnp.sum(cut, axis=1)
            return carry

        lax.fori_loop(0, count // tile, multiply, 0)

    total_modes = fresh * mode
    ones = (
        lax.broadcasted_iota(jnp.int32, (total_modes, lanes), 1) // width
        == lax.broadcasted_iota(jnp.int32, (total_modes, lanes), 0)
    ).astype(jnp.float32)
    partial[me_space] = lax.dot_general(
        ones, picked[...], NT, preferred_element_type=jnp.float32, precision=lax.Precision.HIGHEST
    )
    for k in range(1, space):
        spot = partial.at[me_space]
        copy = pltpu.make_async_remote_copy(
            src_ref=spot, dst_ref=spot, send_sem=sum_send.at[k - 1], recv_sem=sum_recv.at[k - 1],
            device_id={"space": lax.rem(me_space + k, space)}, device_id_type=MESH,
        )
        copy.start()
        sends.append(copy)
    for k in range(1, space):
        source = lax.rem(me_space + space - k, space)
        arrived(partial.at[source], sum_recv.at[k - 1])
    rows_ref[...] = jnp.sum(partial[...], axis=0).T

    for copy in halos:
        copy.wait_send()
    for copy in sends:
        copy.wait_send()
    store_images.wait()


def per_device(space, mode, new_modes, phase_ids, stiffness_table, mode_basis):
    fresh, comps, depth, width, length = new_modes.shape
    count = mode_basis.shape[0]
    chips = mode // 2
    tile = 16
    lanes = fresh * mode * width
    dma = pltpu.SemaphoreType.DMA
    images, rows = pl.pallas_call(
        functools.partial(kernel, space, mode, tile),
        out_shape=(
            jax.ShapeDtypeStruct(new_modes.shape, jnp.bfloat16),
            jax.ShapeDtypeStruct((count, fresh * mode), jnp.float32),
        ),
        in_specs=[pl.BlockSpec(memory_space=pl.ANY)] * 4,
        out_specs=(pl.BlockSpec(memory_space=pl.ANY), pl.BlockSpec(memory_space=pltpu.VMEM)),
        scratch_shapes=[
            pltpu.VMEM((fresh, comps, depth + 2, width, length), jnp.bfloat16),
            pltpu.VMEM((depth, width, length), jnp.int32),
            pltpu.SMEM((3, 3, 2, 27), jnp.float32),
            pltpu.VMEM(mode_basis.shape, jnp.bfloat16),
            pltpu.VMEM((18 * width, 9 * width), jnp.bfloat16),
            pltpu.VMEM((18 * width, 9 * width), jnp.bfloat16),
            pltpu.VMEM((mode, depth, comps, fresh, width, length), jnp.bfloat16),
            pltpu.VMEM((fresh, comps, depth, width, length), jnp.bfloat16),
            pltpu.VMEM((count // tile, tile * width, lanes), jnp.float32),
            pltpu.VMEM((count, lanes), jnp.float32),
            pltpu.VMEM((space, fresh * mode, count), jnp.float32),
            dma((4,)),
            dma,
            dma((2,)),
            dma((2,)),
            dma((depth, chips - 1)),
            dma((depth, chips - 1)),
            dma((depth,)),
            dma((depth,)),
            dma((depth, chips - 1)),
            dma((depth, chips - 1)),
            dma((space - 1,)),
            dma((space - 1,)),
            dma,
        ],
        compiler_params=pltpu.CompilerParams(
            collective_id=0, has_side_effects=True, vmem_limit_bytes=48 * 1024 * 1024
        ),
    )(new_modes, phase_ids, jnp.transpose(stiffness_table, (2, 3, 0, 1)), mode_basis)
    return images, rows


def solution(mesh):
    in_specs = (
        P(("groups", "mode"), None, "space", None, None),
        P(("groups", "space"), None, None),
        P(),
        P(("groups", "mode"), None, "space", None, None),
    )
    out_specs = (P(("groups", "mode"), None, "space", None, None), P(("groups", "mode"), None))
    return jax.shard_map(
        functools.partial(per_device, mesh.shape["space"], mesh.shape["mode"]),
        mesh=mesh, in_specs=in_specs, out_specs=out_specs, check_vma=False,
    )
```

```python
import functools

import jax
import jax.numpy as jnp
from jax import lax
from jax.experimental import pallas as pl
from jax.experimental.pallas import tpu as pltpu
from jax.sharding import PartitionSpec as P

MESH = pl.DeviceIdType.MESH
NT = (((1,), (1,)), ((), ()))


def kernel(
    space, mode, tile,
    modes_hbm, phase_hbm, table_hbm, basis_hbm, images_hbm, rows_ref,
    padded, phase, table, basis, band_hi, band_lo, gathered, own, product, picked, partial,
    load_sem, basis_sem, halo_send, halo_recv, image_send, image_recv, core_send, core_recv,
    pass_send, pass_recv, sum_send, sum_recv, out_sem,
):
    fresh, _, depth, width, _ = modes_hbm.shape
    count = basis_hbm.shape[0]
    chips = mode // 2
    me_space = lax.axis_index("space")
    me = lax.axis_index("mode")
    chip, core = me // 2, lax.rem(me, 2)
    sibling = chip * 2 + (1 - core)
    across = [lax.rem(chip + k, chips) * 2 + core for k in range(1, chips)]
    behind = [lax.rem(chip + chips - k, chips) * 2 + core for k in range(1, chips)]
    up = lax.rem(me_space + 1, space)
    down = lax.rem(me_space + space - 1, space)
    order = list(range(1, depth - 1)) + [0, depth - 1]
    passes = [order[k : k + 2] for k in range(0, depth, 2)]

    load_table = pltpu.make_async_copy(table_hbm, table, load_sem.at[0])
    load_modes = pltpu.make_async_copy(modes_hbm, padded.at[:, :, pl.ds(1, depth)], load_sem.at[1])
    load_phase = pltpu.make_async_copy(phase_hbm, phase, load_sem.at[2])
    load_table.start()
    load_modes.start()
    load_phase.start()

    barrier = pltpu.get_barrier_semaphore()
    for k in range(1, space):
        pl.semaphore_signal(
            barrier, inc=1, device_id={"space": lax.rem(me_space + k, space)}, device_id_type=MESH
        )
    for peer in across + [sibling]:
        pl.semaphore_signal(barrier, inc=1, device_id={"mode": peer}, device_id_type=MESH)

    load_basis = pltpu.make_async_copy(basis_hbm, basis, basis_sem)
    load_basis.start()

    load_table.wait()
    columns = 9 * width
    lane = lax.broadcasted_iota(jnp.int32, (width, columns), 1)
    row = lax.broadcasted_iota(jnp.int32, (width, columns), 0)
    block = lane // width
    offset = lax.rem(lane - row + columns + 1, width)

    def build(q, carry):
        step_y, which, comp = q // 6, lax.rem(q // 3, 2), lax.rem(q, 3)
        total = jnp.zeros((width, columns), jnp.float32)
        for step_x in range(3):
            value = jnp.zeros((width, columns), jnp.float32)
            for inner in range(3):
                for step_z in range(3):
                    coef = table[comp, inner, which, 9 * step_z + 3 * step_x + step_y]
                    value = jnp.where(block == 3 * inner + step_z, coef, value)
            total = jnp.where(offset == step_x, value, total)
        high = total.astype(jnp.bfloat16)
        at = pl.ds(pl.multiple_of(q * width, width), width)
        band_hi[at, :] = high
        band_lo[at, :] = (total - high.astype(jnp.float32)).astype(jnp.bfloat16)
        return carry

    lax.fori_loop(0, 18, build, 0)

    pl.semaphore_wait(barrier, space - 1 + len(across) + 1)

    halos = []
    for side, (layer, target, slot) in enumerate(((depth - 1, up, 0), (0, down, depth + 1))):
        copy = pltpu.make_async_remote_copy(
            src_ref=modes_hbm.at[:, :, pl.ds(layer, 1)],
            dst_ref=padded.at[:, :, pl.ds(slot, 1)],
            send_sem=halo_send.at[side],
            recv_sem=halo_recv.at[side],
            device_id={"space": target},
            device_id_type=MESH,
        )
        copy.start()
        halos.append(copy)

    load_modes.wait()
    load_phase.wait()

    sends = []

    def layer_images(z):
        field = jnp.concatenate(
            [padded[n, :, z : z + 3].reshape(columns, 128) for n in range(fresh)], axis=1
        )
        sums = jnp.dot(band_hi[...], field, preferred_element_type=jnp.float32)
        sums = sums + jnp.dot(band_lo[...], field, preferred_element_type=jnp.float32)
        ids = phase[z]
        masks = [pltpu.roll(ids, shift, 1) == 1 if shift else ids == 1 for shift in (127, 0, 1)]
        for n in range(fresh):
            for comp in range(3):
                result = None
                for step_y, back in ((1, 0), (0, 1), (2, 127)):
                    first = (6 * step_y + comp) * width
                    second = first + 3 * width
                    lanes = slice(n * 128, (n + 1) * 128)
                    term = jnp.where(
                        masks[step_y], sums[second : second + width, lanes], sums[first : first + width, lanes]
                    )
                    term = pltpu.roll(term, back, 1) if back else term
                    result = term if result is None else result + term
                image = result.astype(jnp.bfloat16)
                gathered[me, z, comp, n] = image
                own[n, comp, z] = image

    def send_layer(z):
        spot = gathered.at[me, pl.ds(z, 1)]
        for k, peer in enumerate(across):
            copy = pltpu.make_async_remote_copy(
                src_ref=spot, dst_ref=spot, send_sem=image_send.at[z, k], recv_sem=image_recv.at[z, k],
                device_id={"mode": peer}, device_id_type=MESH,
            )
            copy.start()
            sends.append(copy)
        copy = pltpu.make_async_remote_copy(
            src_ref=spot, dst_ref=spot, send_sem=core_send.at[z], recv_sem=core_recv.at[z],
            device_id={"mode": sibling}, device_id_type=MESH,
        )
        copy.start()
        sends.append(copy)

    def arrived(spot, sem):
        pltpu.make_async_remote_copy(
            src_ref=spot, dst_ref=spot, send_sem=out_sem, recv_sem=sem,
            device_id={"mode": sibling}, device_id_type=MESH,
        ).wait_recv()

    def pass_layer(z):
        for k, source in enumerate(behind):
            spot = gathered.at[source, pl.ds(z, 1)]
            arrived(spot, image_recv.at[z, k])
            copy = pltpu.make_async_remote_copy(
                src_ref=spot, dst_ref=spot, send_sem=pass_send.at[z, k], recv_sem=pass_recv.at[z, k],
                device_id={"mode": sibling}, device_id_type=MESH,
            )
            copy.start()
            sends.append(copy)

    for z in order:
        if z == 0:
            for copy in halos:
                copy.wait_recv()
        layer_images(z)
        send_layer(z)

    store_images = pltpu.make_async_copy(own, images_hbm, load_sem.at[3])
    store_images.start()

    lanes = fresh * mode * width
    spread = lax.broadcasted_iota(jnp.int32, (width, lanes), 1)
    keep = lax.rem(spread, width) == lax.broadcasted_iota(jnp.int32, (width, lanes), 0)
    for number, layers in enumerate(passes):
        for z in layers:
            pass_layer(z)
        if number == 0:
            load_basis.wait()
        for z in layers:
            arrived(gathered.at[sibling, pl.ds(z, 1)], core_recv.at[z])
            for k, source in enumerate(behind):
                other = source + 1 - 2 * core
                arrived(gathered.at[other, pl.ds(z, 1)], pass_recv.at[z, k])

        def multiply(t, carry):
            at = pl.ds(t * tile, tile)
            left = jnp.concatenate(
                [basis[at, c, z].reshape(tile * width, 128) for z in layers for c in range(3)], axis=1
            )
            right = jnp.concatenate(
                [gathered[:, z, c].reshape(lanes, 128) for z in layers for c in range(3)], axis=1
            )
            value = lax.dot_general(left, right, NT, preferred_element_type=jnp.float32)
            if number > 0:
                value = value + product[t]
            if number < len(passes) - 1:
                product[t] = value
            else:
                cut = jnp.where(keep[None], value.reshape(tile, width, lanes), 0.0)
                picked[pl.ds(pl.multiple_of(t * tile, tile), tile), :] = jnp.sum(cut, axis=1)
            return carry

        lax.fori_loop(0, count // tile, multiply, 0)

    total_modes = fresh * mode
    ones = (
        lax.broadcasted_iota(jnp.int32, (total_modes, lanes), 1) // width
        == lax.broadcasted_iota(jnp.int32, (total_modes, lanes), 0)
    ).astype(jnp.float32)
    partial[me_space] = lax.dot_general(
        ones, picked[...], NT, preferred_element_type=jnp.float32, precision=lax.Precision.HIGHEST
    )
    for k in range(1, space):
        spot = partial.at[me_space]
        copy = pltpu.make_async_remote_copy(
            src_ref=spot, dst_ref=spot, send_sem=sum_send.at[k - 1], recv_sem=sum_recv.at[k - 1],
            device_id={"space": lax.rem(me_space + k, space)}, device_id_type=MESH,
        )
        copy.start()
        sends.append(copy)
    for k in range(1, space):
        source = lax.rem(me_space + space - k, space)
        arrived(partial.at[source], sum_recv.at[k - 1])
    rows_ref[...] = jnp.sum(partial[...], axis=0)

    for copy in halos:
        copy.wait_send()
    for copy in sends:
        copy.wait_send()
    store_images.wait()


def per_device(space, mode, new_modes, phase_ids, stiffness_table, mode_basis):
    fresh, comps, depth, width, length = new_modes.shape
    count = mode_basis.shape[0]
    chips = mode // 2
    tile = min(64, count)
    lanes = fresh * mode * width
    dma = pltpu.SemaphoreType.DMA
    images, rows = pl.pallas_call(
        functools.partial(kernel, space, mode, tile),
        out_shape=(
            jax.ShapeDtypeStruct(new_modes.shape, jnp.bfloat16),
            jax.ShapeDtypeStruct((fresh * mode, count), jnp.float32),
        ),
        in_specs=[pl.BlockSpec(memory_space=pltpu.HBM)] * 4,
        out_specs=(pl.BlockSpec(memory_space=pltpu.HBM), pl.BlockSpec(memory_space=pltpu.VMEM)),
        scratch_shapes=[
            pltpu.VMEM((fresh, comps, depth + 2, width, length), jnp.bfloat16),
            pltpu.VMEM((depth, width, length), jnp.int32),
            pltpu.SMEM((3, 3, 2, 27), jnp.float32),
            pltpu.VMEM(mode_basis.shape, jnp.bfloat16),
            pltpu.VMEM((18 * width, 9 * width), jnp.bfloat16),
            pltpu.VMEM((18 * width, 9 * width), jnp.bfloat16),
            pltpu.VMEM((mode, depth, comps, fresh, width, length), jnp.bfloat16),
            pltpu.VMEM((fresh, comps, depth, width, length), jnp.bfloat16),
            pltpu.VMEM((count // tile, tile * width, lanes), jnp.float32),
            pltpu.VMEM((count, lanes), jnp.float32),
            pltpu.VMEM((space, fresh * mode, count), jnp.float32),
            dma((4,)),
            dma,
            dma((2,)),
            dma((2,)),
            dma((depth, chips - 1)),
            dma((depth, chips - 1)),
            dma((depth,)),
            dma((depth,)),
            dma((depth, chips - 1)),
            dma((depth, chips - 1)),
            dma((space - 1,)),
            dma((space - 1,)),
            dma,
        ],
        compiler_params=pltpu.CompilerParams(
            collective_id=0, has_side_effects=True, vmem_limit_bytes=48 * 1024 * 1024
        ),
    )(*(
        pltpu.with_memory_space_constraint(a, pltpu.HBM)
        for a in (new_modes, phase_ids, jnp.transpose(stiffness_table, (2, 3, 0, 1)), mode_basis)
    ))
    return images, rows.T


def solution(mesh):
    in_specs = (
        P(("groups", "mode"), None, "space", None, None),
        P(("groups", "space"), None, None),
        P(),
        P(("groups", "mode"), None, "space", None, None),
    )
    out_specs = (P(("groups", "mode"), None, "space", None, None), P(("groups", "mode"), None))
    return jax.shard_map(
        functools.partial(per_device, mesh.shape["space"], mesh.shape["mode"]),
        mesh=mesh, in_specs=in_specs, out_specs=out_specs, check_vma=False,
    )
```

```python
import functools

import jax
import jax.numpy as jnp
from jax import lax
from jax.experimental import pallas as pl
from jax.experimental.pallas import tpu as pltpu
from jax.sharding import PartitionSpec as P

MESH = pl.DeviceIdType.MESH
NT = (((1,), (1,)), ((), ()))


def kernel(
    space, mode, tile,
    modes_hbm, phase_hbm, table_hbm, basis_hbm, images_hbm, rows_ref,
    padded, phase, table, basis, band_hi, band_lo, gathered, own, product, picked, partial,
    load_sem, basis_sem, halo_send, halo_recv, image_send, image_recv, core_send, core_recv,
    pass_send, pass_recv, sum_send, sum_recv, out_sem,
):
    fresh, _, depth, width, _ = modes_hbm.shape
    count = basis_hbm.shape[0]
    chips = mode // 2
    me_space = lax.axis_index("space")
    me = lax.axis_index("mode")
    chip, core = me // 2, lax.rem(me, 2)
    sibling = chip * 2 + (1 - core)
    across = [lax.rem(chip + k, chips) * 2 + core for k in range(1, chips)]
    behind = [lax.rem(chip + chips - k, chips) * 2 + core for k in range(1, chips)]
    up = lax.rem(me_space + 1, space)
    down = lax.rem(me_space + space - 1, space)
    inner = list(range(1, depth - 1))
    first_edge = jnp.where(me_space == 0, depth - 1, 0)
    edges = [first_edge, depth - 1 - first_edge]
    passes = [inner[k : k + 2] for k in range(0, depth - 2, 2)] + [edges]

    load_table = pltpu.make_async_copy(table_hbm, table, load_sem.at[0])
    load_modes = pltpu.make_async_copy(modes_hbm, padded.at[:, :, pl.ds(1, depth)], load_sem.at[1])
    load_phase = pltpu.make_async_copy(phase_hbm, phase, load_sem.at[2])
    load_table.start()
    load_modes.start()
    load_phase.start()

    barrier = pltpu.get_barrier_semaphore()
    for k in range(1, space):
        pl.semaphore_signal(
            barrier, inc=1, device_id={"space": lax.rem(me_space + k, space)}, device_id_type=MESH
        )
    for peer in across + [sibling]:
        pl.semaphore_signal(barrier, inc=1, device_id={"mode": peer}, device_id_type=MESH)

    load_basis = pltpu.make_async_copy(basis_hbm, basis, basis_sem)
    load_basis.start()

    load_table.wait()
    columns = 9 * width
    lane = lax.broadcasted_iota(jnp.int32, (width, columns), 1)
    row = lax.broadcasted_iota(jnp.int32, (width, columns), 0)
    block = lane // width
    offset = lax.rem(lane - row + columns + 1, width)

    def build(q, carry):
        step_y, which, comp = q // 6, lax.rem(q // 3, 2), lax.rem(q, 3)
        total = jnp.zeros((width, columns), jnp.float32)
        for step_x in range(3):
            value = jnp.zeros((width, columns), jnp.float32)
            for inner in range(3):
                for step_z in range(3):
                    coef = table[comp, inner, which, 9 * step_z + 3 * step_x + step_y]
                    value = jnp.where(block == 3 * inner + step_z, coef, value)
            total = jnp.where(offset == step_x, value, total)
        high = total.astype(jnp.bfloat16)
        at = pl.ds(pl.multiple_of(q * width, width), width)
        band_hi[at, :] = high
        band_lo[at, :] = (total - high.astype(jnp.float32)).astype(jnp.bfloat16)
        return carry

    lax.fori_loop(0, 18, build, 0)

    pl.semaphore_wait(barrier, space - 1 + len(across) + 1)

    halos = []
    for side, (layer, target, slot) in enumerate(((depth - 1, up, 0), (0, down, depth + 1))):
        copy = pltpu.make_async_remote_copy(
            src_ref=modes_hbm.at[:, :, pl.ds(layer, 1)],
            dst_ref=padded.at[:, :, pl.ds(slot, 1)],
            send_sem=halo_send.at[side],
            recv_sem=halo_recv.at[side],
            device_id={"space": target},
            device_id_type=MESH,
        )
        copy.start()
        halos.append(copy)

    load_modes.wait()
    load_phase.wait()

    sends = []

    def layer_images(z):
        field = jnp.concatenate(
            [padded[n, :, pl.ds(z, 3)].reshape(columns, 128) for n in range(fresh)], axis=1
        )
        sums = jnp.dot(band_hi[...], field, preferred_element_type=jnp.float32)
        sums = sums + jnp.dot(band_lo[...], field, preferred_element_type=jnp.float32)
        ids = phase[z]
        masks = [pltpu.roll(ids, shift, 1) == 1 if shift else ids == 1 for shift in (127, 0, 1)]
        for n in range(fresh):
            for comp in range(3):
                result = None
                for step_y, back in ((1, 0), (0, 1), (2, 127)):
                    first = (6 * step_y + comp) * width
                    second = first + 3 * width
                    lanes = slice(n * 128, (n + 1) * 128)
                    term = jnp.where(
                        masks[step_y], sums[second : second + width, lanes], sums[first : first + width, lanes]
                    )
                    term = pltpu.roll(term, back, 1) if back else term
                    result = term if result is None else result + term
                image = result.astype(jnp.bfloat16)
                gathered[me, z, comp, n] = image
                own[n, comp, z] = image

    def send_layer(z):
        spot = gathered.at[me, pl.ds(z, 1)]
        for k, peer in enumerate(across):
            copy = pltpu.make_async_remote_copy(
                src_ref=spot, dst_ref=spot, send_sem=image_send.at[z, k], recv_sem=image_recv.at[z, k],
                device_id={"mode": peer}, device_id_type=MESH,
            )
            copy.start()
            sends.append(copy)
        copy = pltpu.make_async_remote_copy(
            src_ref=spot, dst_ref=spot, send_sem=core_send.at[z], recv_sem=core_recv.at[z],
            device_id={"mode": sibling}, device_id_type=MESH,
        )
        copy.start()
        sends.append(copy)

    def arrived(spot, sem):
        pltpu.make_async_remote_copy(
            src_ref=spot, dst_ref=spot, send_sem=out_sem, recv_sem=sem,
            device_id={"mode": sibling}, device_id_type=MESH,
        ).wait_recv()

    def pass_layer(z):
        for k, source in enumerate(behind):
            spot = gathered.at[source, pl.ds(z, 1)]
            arrived(spot, image_recv.at[z, k])
            copy = pltpu.make_async_remote_copy(
                src_ref=spot, dst_ref=spot, send_sem=pass_send.at[z, k], recv_sem=pass_recv.at[z, k],
                device_id={"mode": sibling}, device_id_type=MESH,
            )
            copy.start()
            sends.append(copy)

    for z in inner:
        layer_images(z)
        send_layer(z)
    for z in edges:
        side = z // (depth - 1)
        arrived(padded.at[:, :, pl.ds(side * (depth + 1), 1)], halo_recv.at[side])
        layer_images(z)
        send_layer(z)

    store_images = pltpu.make_async_copy(own, images_hbm, load_sem.at[3])
    store_images.start()

    lanes = fresh * mode * width
    spread = lax.broadcasted_iota(jnp.int32, (width, lanes), 1)
    keep = lax.rem(spread, width) == lax.broadcasted_iota(jnp.int32, (width, lanes), 0)
    for number, layers in enumerate(passes):
        for z in layers:
            pass_layer(z)
        if number == 0:
            load_basis.wait()
        for z in layers:
            arrived(gathered.at[sibling, pl.ds(z, 1)], core_recv.at[z])
            for k, source in enumerate(behind):
                other = source + 1 - 2 * core
                arrived(gathered.at[other, pl.ds(z, 1)], pass_recv.at[z, k])

        def multiply(t, carry):
            at = pl.ds(t * tile, tile)
            left = jnp.concatenate(
                [basis[at, c, z].reshape(tile * width, 128) for z in layers for c in range(3)], axis=1
            )
            right = jnp.concatenate(
                [gathered[:, z, c].reshape(lanes, 128) for z in layers for c in range(3)], axis=1
            )
            value = lax.dot_general(left, right, NT, preferred_element_type=jnp.float32)
            if number > 0:
                value = value + product[t]
            if number < len(passes) - 1:
                product[t] = value
            else:
                cut = jnp.where(keep[None], value.reshape(tile, width, lanes), 0.0)
                picked[pl.ds(pl.multiple_of(t * tile, tile), tile), :] = jnp.sum(cut, axis=1)
            return carry

        lax.fori_loop(0, count // tile, multiply, 0, unroll=True)

    total_modes = fresh * mode
    ones = (
        lax.broadcasted_iota(jnp.int32, (total_modes, lanes), 1) // width
        == lax.broadcasted_iota(jnp.int32, (total_modes, lanes), 0)
    ).astype(jnp.float32)
    partial[me_space] = lax.dot_general(
        ones, picked[...], NT, preferred_element_type=jnp.float32, precision=lax.Precision.HIGHEST
    )
    for k in range(1, space):
        spot = partial.at[me_space]
        copy = pltpu.make_async_remote_copy(
            src_ref=spot, dst_ref=spot, send_sem=sum_send.at[k - 1], recv_sem=sum_recv.at[k - 1],
            device_id={"space": lax.rem(me_space + k, space)}, device_id_type=MESH,
        )
        copy.start()
        sends.append(copy)
    for k in range(1, space):
        source = lax.rem(me_space + space - k, space)
        arrived(partial.at[source], sum_recv.at[k - 1])
    rows_ref[...] = jnp.sum(partial[...], axis=0)

    for copy in halos:
        copy.wait_send()
    for copy in sends:
        copy.wait_send()
    store_images.wait()


def per_device(space, mode, new_modes, phase_ids, stiffness_table, mode_basis):
    fresh, comps, depth, width, length = new_modes.shape
    count = mode_basis.shape[0]
    chips = mode // 2
    tile = min(64, count)
    lanes = fresh * mode * width
    dma = pltpu.SemaphoreType.DMA
    images, rows = pl.pallas_call(
        functools.partial(kernel, space, mode, tile),
        out_shape=(
            jax.ShapeDtypeStruct(new_modes.shape, jnp.bfloat16),
            jax.ShapeDtypeStruct((fresh * mode, count), jnp.float32),
        ),
        in_specs=[pl.BlockSpec(memory_space=pltpu.HBM)] * 4,
        out_specs=(pl.BlockSpec(memory_space=pltpu.HBM), pl.BlockSpec(memory_space=pltpu.VMEM)),
        scratch_shapes=[
            pltpu.VMEM((fresh, comps, depth + 2, width, length), jnp.bfloat16),
            pltpu.VMEM((depth, width, length), jnp.int32),
            pltpu.SMEM((3, 3, 2, 27), jnp.float32),
            pltpu.VMEM(mode_basis.shape, jnp.bfloat16),
            pltpu.VMEM((18 * width, 9 * width), jnp.bfloat16),
            pltpu.VMEM((18 * width, 9 * width), jnp.bfloat16),
            pltpu.VMEM((mode, depth, comps, fresh, width, length), jnp.bfloat16),
            pltpu.VMEM((fresh, comps, depth, width, length), jnp.bfloat16),
            pltpu.VMEM((count // tile, tile * width, lanes), jnp.float32),
            pltpu.VMEM((count, lanes), jnp.float32),
            pltpu.VMEM((space, fresh * mode, count), jnp.float32),
            dma((4,)),
            dma,
            dma((2,)),
            dma((2,)),
            dma((depth, chips - 1)),
            dma((depth, chips - 1)),
            dma((depth,)),
            dma((depth,)),
            dma((depth, chips - 1)),
            dma((depth, chips - 1)),
            dma((space - 1,)),
            dma((space - 1,)),
            dma,
        ],
        compiler_params=pltpu.CompilerParams(
            collective_id=0, has_side_effects=True, vmem_limit_bytes=48 * 1024 * 1024
        ),
    )(*(
        pltpu.with_memory_space_constraint(a, pltpu.HBM)
        for a in (new_modes, phase_ids, jnp.transpose(stiffness_table, (2, 3, 0, 1)), mode_basis)
    ))
    return images, rows.T


def solution(mesh):
    in_specs = (
        P(("groups", "mode"), None, "space", None, None),
        P(("groups", "space"), None, None),
        P(),
        P(("groups", "mode"), None, "space", None, None),
    )
    out_specs = (P(("groups", "mode"), None, "space", None, None), P(("groups", "mode"), None))
    return jax.shard_map(
        functools.partial(per_device, mesh.shape["space"], mesh.shape["mode"]),
        mesh=mesh, in_specs=in_specs, out_specs=out_specs, check_vma=False,
    )
```
